32 devices in a mesh: src: 8 (over z, y), att: 4 (over x, core).
Axes of the slice: x: 2, y: 2, z: 4, core: 2. Of those that a mesh axis runs over, the one named last changes fastest.
Arguments:
- astro: float32 [5, 4096], P(None, 'src'), may hold values from -6 to 6
- attitude: float32 [196608], P('att'), may hold values from -6 to 6
- spline_weights: bfloat16 [2048, 64, 128], P(('src', 'att')), may hold values from -0.75 to 0.75
- source_coeffs: bfloat16 [2048, 5, 128], P(('src', 'att')), may hold values from -2.5 to 2.5
- observations: float32 [2048, 128], P(('src', 'att')), may hold values from -12 to 12
- knot_start: int32 [2048], P(('src', 'att')), may hold values from 0 to 49088
- block_count: int32 [4, 32], P('att', 'src'), may hold values from 1 to 16, as said below
Outputs:
- astro_new: float32 [5, 4096], P(None, 'src')
- attitude_new: float32 [196608], P('att')
The draws below stay inside these ranges and needn't reach their ends.
Inputs may be any that keep to these rules, and one draw needn't show every extreme that they name: `block_count`: A block's live tiles fill its slots 0 to count - 1 at that owner; the other slots hold entries that no output reads. Some block has all 16 slots live.
All inputs are finite; a program needn't handle non-finite values.
Results may differ from the reference program's by a relative error of at most 0.0003.
Values sent between devices are 32-bit elements; how exact they have to be, the bound alone decides.
A program may use at most 64 MiB of HBM per device.

```python
import jax
import jax.numpy as jnp
from jax import lax

NB = 128
P_SIZE = 5
KS = 64
BLK_DEV = 4
TPB = 16
SEG_ATT = 768
PASSES = 2
BLOCKS = 32
SOURCES = 4096
KNOTS = 196608
TILES = 2048
N_ATT = 4


def draw_observations(key, part):
    row_pos = jnp.arange(TILES, dtype=jnp.float32)[:, None]
    scale = 1.0 + 2.0 * row_pos / TILES
    base_draw = jnp.clip(jax.random.normal(key, (TILES, NB), jnp.float32), -4.0, 4.0)
    return base_draw * scale


def draw_block_count(key, part):
    src_count = BLOCKS // BLK_DEV
    key_base = jax.random.fold_in(key, 11)
    key_device = jax.random.fold_in(key, 23)
    base_draw = jax.random.randint(key_base, (N_ATT, BLOCKS), 0, TPB)
    factor = jax.random.randint(key_device, (N_ATT, src_count, 1), 1, 5)
    factor = jnp.broadcast_to(factor, (N_ATT, src_count, BLK_DEV)).reshape(N_ATT, BLOCKS)
    counts = 1 + base_draw * factor // 4
    return counts.at[0, 0].set(TPB).astype(jnp.int32)


def place_ends(drawn, rng, low, high):
    longest = drawn.shape.index(max(drawn.shape))
    spots = []
    for shift in (0, 1):
        where = [jax.random.randint(jax.random.fold_in(rng, axis), (), 0, length) for axis, length in enumerate(drawn.shape)]
        where[longest] = (where[longest] + shift) % drawn.shape[longest]
        spots.append(tuple(where))
    return drawn.at[spots[0]].set(low).at[spots[1]].set(high)


def level_of(rng, extent, shards, least, high):
    def one(dim, shards_of):
        heights = jax.random.uniform(jax.random.fold_in(jax.random.fold_in(rng, 6), dim), (shards_of,), jnp.float32, least / len(shards), high / len(shards))
        return jnp.repeat(jnp.exp(heights), extent[dim] // shards_of).reshape((-1,) + (1,) * (len(extent) - dim - 1))

    level = one(*shards[0])
    for cut in shards[1:]:
        level = level * one(*cut)
    return level


def gaussian(stream_key, extent, spread, limit, shards=(), kind=jnp.bfloat16):
    gain = level_of(stream_key, extent, shards, -0.22, 0.18) if shards else 1.0
    result = jax.random.normal(stream_key, extent, jnp.float32) * spread * gain
    return jnp.minimum(jnp.maximum(result, -limit), limit).astype(kind)


def setup_inputs(seed: int = 0) -> dict:
    splits = jax.random.split(jax.random.key(seed), 8)
    return {
        "astro": gaussian(splits[0], (P_SIZE, SOURCES), 1.0, 6.0, ((1, 8),), jnp.float32),
        "attitude": gaussian(splits[1], (KNOTS,), 1.0, 6.0, ((0, 4),), jnp.float32),
        "spline_weights": gaussian(splits[2], (TILES, KS, NB), KS ** -0.5, 0.75, ((0, 32),)),
        "source_coeffs": gaussian(splits[3], (TILES, P_SIZE, NB), P_SIZE ** -0.5, 2.5, ((0, 32),)),
        "observations": draw_observations(jax.random.fold_in(splits[7], 71), 0),
        "knot_start": place_ends(jax.random.randint(splits[5], (TILES,), 0, SEG_ATT * KS - KS + 1), jax.random.fold_in(splits[5], 1), 0, SEG_ATT * KS - KS).astype(jnp.int32),
        "block_count": draw_block_count(jax.random.fold_in(splits[7], 71), 0),
    }


damping = 1.0


def attitude_model(weights, window):
    return jnp.sum(weights.astype(jnp.float32) * window[..., None], axis=-2)


def source_model(coeffs, params):
    return jnp.sum(coeffs.astype(jnp.float32) * params, axis=-2)


def reference(astro, attitude, spline_weights, source_coeffs, observations, knot_start, block_count):
    src_count = BLOCKS // BLK_DEV
    knot_att = SEG_ATT * KS
    weights = spline_weights.reshape(src_count, N_ATT, BLK_DEV, TPB, KS, NB)
    coeffs = source_coeffs.reshape(src_count, N_ATT, BLK_DEV, TPB, P_SIZE, NB)
    observed = observations.reshape(src_count, N_ATT, BLK_DEV, TPB, NB)
    starts = knot_start.reshape(src_count, N_ATT, BLK_DEV, TPB)
    counts = jnp.transpose(block_count.reshape(N_ATT, src_count, BLK_DEV), (1, 0, 2))
    params = jnp.transpose(astro.reshape(P_SIZE, src_count, BLK_DEV, NB), (1, 2, 0, 3))
    attitude_rows = attitude.reshape(N_ATT, knot_att)
    owners = jnp.arange(N_ATT, dtype=jnp.int32)[:, None, None, None]
    offsets = jnp.arange(KS, dtype=jnp.int32)
    slot_ids = jnp.arange(TPB, dtype=jnp.int32)

    def live_of(count_rows):
        return (slot_ids[None, None, :] < count_rows[:, :, None]).astype(jnp.float32)

    def positions_of(start_rows):
        knot_ids = start_rows[..., None].astype(jnp.int32) + offsets
        return jnp.broadcast_to(owners, knot_ids.shape), knot_ids

    def residual(tiles, block_params, rows_now):
        part_w, part_c, part_y, part_s, part_n = tiles
        owner_ids, knot_ids = positions_of(part_s)
        window = rows_now[owner_ids, knot_ids]
        predicted = source_model(part_c, block_params[None, :, None]) + attitude_model(part_w, window)
        return (part_y - predicted) * live_of(part_n)[..., None]

    tile_xs = (weights, coeffs, observed, starts, counts)

    def source_square(tiles):
        part_w, part_c, part_y, part_s, part_n = tiles
        live = live_of(part_n)
        return jnp.sum(jnp.square(part_c.astype(jnp.float32)) * live[..., None, None], axis=(0, 2))

    source_diag = lax.map(source_square, tile_xs) + damping

    def knot_square(totals, tiles):
        part_w, part_c, part_y, part_s, part_n = tiles
        values = jnp.sum(jnp.square(part_w.astype(jnp.float32)), axis=-1) * live_of(part_n)[..., None]
        owner_ids, knot_ids = positions_of(part_s)
        return totals.at[owner_ids, knot_ids].add(values), None

    knot_diag = lax.scan(knot_square, jnp.zeros((N_ATT, knot_att), jnp.float32), tile_xs)[0] + damping

    for pass_no in range(PASSES):
        rows_now = attitude_rows

        def source_gradient(inputs):
            tiles, block_params = inputs[:5], inputs[5]
            resid = residual(tiles, block_params, rows_now)
            return jnp.sum(tiles[1].astype(jnp.float32) * resid[..., None, :], axis=(0, 2))

        gradient = lax.map(source_gradient, tile_xs + (params,))
        params = params + gradient / source_diag

        def knot_gradient(totals, inputs):
            tiles, block_params = inputs[:5], inputs[5]
            resid = residual(tiles, block_params, rows_now)
            values = jnp.sum(tiles[0].astype(jnp.float32) * resid[..., None, :], axis=-1)
            owner_ids, knot_ids = positions_of(tiles[3])
            return totals.at[owner_ids, knot_ids].add(values), None

        knot_total = lax.scan(knot_gradient, jnp.zeros((N_ATT, knot_att), jnp.float32), tile_xs + (params,))[0]
        attitude_rows = rows_now + knot_total / knot_diag

    astro_new = jnp.transpose(params, (2, 0, 1, 3)).reshape(P_SIZE, BLOCKS * NB)
    return (astro_new, attitude_rows.reshape(N_ATT * knot_att))
```

```python
import functools

import jax
import jax.numpy as jnp
from jax import lax
from jax.experimental import pallas as pl
from jax.experimental.pallas import tpu as pltpu
from jax.sharding import PartitionSpec as P

PASSES = 2
LANES = 128
GROUP = 4

damping = 1.0

F32 = jnp.float32
BF16 = jnp.bfloat16
MESH = pl.DeviceIdType.MESH


def split(value):
    high = value.astype(BF16)
    low = (value - high.astype(F32)).astype(BF16)
    return high, low


def dot(a, b):
    return jnp.dot(a, b, preferred_element_type=F32)


def dot_rows(a, b):
    return lax.dot_general(a, b, (((1,), (1,)), ((), ())), preferred_element_type=F32)


def kernel(
    n_src, n_att, blocks, slots, knots, params, rows,
    astro_ref, attitude_ref, w_ref, c_ref, y_ref, start_ref, count_ref,
    x_out, a_out,
    planes, coeffs32, hot, pick, offs, starts, acc, inv, att_first, att_later, sq_buf, grad_buf,
    att_send, att_recv, src_send, src_recv,
):
    tiles = blocks * slots
    wide = slots * knots
    src = lax.axis_index("src")
    att = lax.axis_index("att")

    barrier = pltpu.get_barrier_semaphore()

    def greet_src(step, carry):
        pl.semaphore_signal(barrier, inc=1, device_id=(lax.rem(src + step, n_src), att), device_id_type=MESH)
        return carry

    def greet_att(step, carry):
        pl.semaphore_signal(barrier, inc=1, device_id=(src, lax.rem(att + step, n_att)), device_id_type=MESH)
        return carry

    lax.fori_loop(1, n_att, greet_att, 0)
    lax.fori_loop(1, n_src, greet_src, 0)

    def send_src(buf, which):
        def step_fn(step, carry):
            pltpu.make_async_remote_copy(
                src_ref=buf.at[src], dst_ref=buf.at[src],
                send_sem=src_send.at[which], recv_sem=src_recv.at[which],
                device_id=(lax.rem(src + step, n_src), att), device_id_type=MESH,
            ).start()
            return carry

        lax.fori_loop(1, n_src, step_fn, 0)

    def send_att(buf, which):
        def step_fn(step, carry):
            pltpu.make_async_remote_copy(
                src_ref=buf.at[att], dst_ref=buf.at[att],
                send_sem=att_send.at[which], recv_sem=att_recv.at[which],
                device_id=(src, lax.rem(att + step, n_att)), device_id_type=MESH,
            ).start()
            return carry

        lax.fori_loop(1, n_att, step_fn, 0)

    def wait_bytes(buf, count, sem):
        part = buf.at[pl.ds(0, count)]
        pltpu.make_async_copy(part, part, sem).wait()

    row_starts = start_ref[...]
    twice = jnp.broadcast_to(jnp.concatenate([row_starts, row_starts], axis=1), (8, LANES))
    starts[src] = twice
    column = jnp.transpose(twice)[0:tiles, 0:1]
    start = jnp.broadcast_to(column, (tiles, LANES))
    off = jnp.bitwise_and(start, LANES - 1)
    lane = lax.broadcasted_iota(jnp.int32, (tiles, LANES), 1)
    start_row = jnp.broadcast_to(jnp.right_shift(column, 7), (tiles, rows))
    row_id = lax.broadcasted_iota(jnp.int32, (tiles, rows), 1)
    pick[0:tiles, :] = jnp.where(row_id == start_row, 1.0, 0.0).astype(BF16)
    pick[tiles:, :] = jnp.where(row_id == start_row + 1, 1.0, 0.0).astype(BF16)

    coeffs32[:, 0:params, :] = c_ref[...].astype(F32)
    for p in range(params):
        planes[p] = coeffs32[:, p, :]

    slot_id = lax.broadcasted_iota(jnp.int32, (slots, LANES), 0)
    live = [slot_id < count_ref[0, b] for b in range(blocks)]
    own = jnp.right_shift(lax.broadcasted_iota(jnp.int32, (slots, wide), 1), 6) == lax.broadcasted_iota(
        jnp.int32, (slots, wide), 0
    )

    def windows(attitude):
        high, low = split(attitude)
        found = dot(pick[...], jnp.concatenate([high, low], axis=1))
        found = found[:, :LANES] + found[:, LANES:]
        window = jnp.where(lane >= off, found[:tiles], found[tiles:])
        for bit in range(7):
            moved = pltpu.roll(window, LANES - (1 << bit), 1)
            window = jnp.where(jnp.bitwise_and(off, 1 << bit) != 0, moved, window)
        return jnp.where(lane < knots, window, pltpu.roll(window, knots, 1))

    def predict(window):
        found = []
        for b in range(blocks):
            part = window[b * slots : (b + 1) * slots]
            part = jnp.where(own, jnp.concatenate([part] * (wide // LANES), axis=1), 0.0)
            both = dot(jnp.concatenate(split(part), axis=0), w_ref[b * wide : (b + 1) * wide, :])
            found.append(both[:slots] + both[slots:])
        return found

    def residual(x, predicted):
        found = []
        for b in range(blocks):
            total = predicted[b]
            for p in range(params):
                total = total + planes[p, b * slots : (b + 1) * slots, :] * x[p * blocks + b : p * blocks + b + 1, :]
            found.append(jnp.where(live[b], y_ref[b * slots : (b + 1) * slots, :] - total, 0.0))
        return found

    def source_terms(resid):
        return [
            jnp.sum(planes[p, b * slots : (b + 1) * slots, :] * resid[b], axis=0, keepdims=True)
            for p in range(params)
            for b in range(blocks)
        ]

    def source_squares():
        return [
            jnp.sum(jnp.where(live[b], jnp.square(planes[p, b * slots : (b + 1) * slots, :]), 0.0), axis=0, keepdims=True)
            for p in range(params)
            for b in range(blocks)
        ]

    def own_columns(both):
        both = jnp.where(own, both[:slots] + both[slots:], 0.0)
        total = both[:, :LANES]
        for part in range(1, wide // LANES):
            total = total + both[:, part * LANES : (part + 1) * LANES]
        return total + pltpu.roll(total, knots, 1)

    def placed(values):
        values = jnp.concatenate(values, axis=0)
        for bit in range(6):
            moved = pltpu.roll(values, 1 << bit, 1)
            values = jnp.where(jnp.bitwise_and(off, 1 << bit) != 0, moved, values)
        half = tiles // 2
        return jnp.where(lane[:half] < knots, values[:half], values[half:])

    def knot_terms(resid):
        return [
            own_columns(dot_rows(jnp.concatenate(split(resid[b]), axis=0), w_ref[b * wide : (b + 1) * wide, :]))
            for b in range(blocks)
        ]

    def knot_squares():
        ones = jnp.ones((slots, LANES), BF16)
        found = []
        for b in range(blocks):
            high, low = split(jnp.square(w_ref[b * wide : (b + 1) * wide, :].astype(F32)))
            both = jnp.concatenate([dot_rows(ones, high), dot_rows(ones, low)], axis=0)
            found.append(jnp.where(live[b], own_columns(both), 0.0))
        return found

    def prepare(chunk, carry):
        first = chunk * GROUP
        low_half = lax.broadcasted_iota(jnp.int32, (8, LANES), 1) < tiles
        ids = lax.broadcasted_iota(jnp.int32, (rows, LANES), 0)
        for pair in range(GROUP // 2):
            both = jnp.where(low_half, starts[first + 2 * pair], starts[first + 2 * pair + 1])
            both = jnp.broadcast_to(jnp.right_shift(both, 7)[0:1], (rows, LANES))
            hot[chunk, :, pair * LANES : (pair + 1) * LANES] = jnp.where(ids == both, 1.0, 0.0).astype(BF16)
        for d in range(GROUP):
            lanes_of = jnp.transpose(jnp.bitwise_and(starts[first + d], LANES - 1))
            offs[first + d] = jnp.broadcast_to(lanes_of[0:tiles, 0:1], (tiles, LANES))
        return carry

    def group_sum(chunk, buf_of):
        first = chunk * GROUP
        half = tiles // 2
        parts = []
        for d in range(GROUP):
            packed = buf_of(first + d)
            other = pltpu.roll(packed, knots, 1)
            low_half = lane[:half] < knots
            values = jnp.concatenate([jnp.where(low_half, packed, other), jnp.where(low_half, other, packed)], axis=0)
            at = offs[first + d]
            here = jnp.where(jnp.logical_and(lane >= at, lane < at + knots), values, 0.0)
            later = jnp.where(lane < at - knots, values, 0.0)
            parts.append(jnp.concatenate([here, later], axis=1))
        high, low = split(jnp.concatenate(parts, axis=0))
        return dot(hot[chunk], high) + dot(hot[chunk], low)

    n_groups = n_src // GROUP

    def over_groups(buf_of):
        if n_groups <= 2:
            total = group_sum(0, buf_of)
            for chunk in range(1, n_groups):
                total = total + group_sum(chunk, buf_of)
        else:
            acc[...] = jnp.zeros_like(acc)

            def step_fn(chunk, carry):
                acc[...] += group_sum(chunk, buf_of)
                return carry

            lax.fori_loop(0, n_groups, step_fn, 0)
            total = acc[...]
        return total[:, :LANES] + pltpu.roll(total[:, LANES:], 1, 0)

    x = jnp.concatenate(
        [astro_ref[p : p + 1, b * LANES : (b + 1) * LANES] for p in range(params) for b in range(blocks)], axis=0
    )
    count = params * blocks
    attitude = attitude_ref[...]
    for turn in range(PASSES):
        predicted = predict(windows(attitude))
        terms = source_terms(residual(x, predicted))
        if turn == 0:
            att_first[att] = jnp.concatenate(terms + source_squares(), axis=0)
            pl.semaphore_wait(barrier, n_src + n_att - 2)
            send_att(att_first, 0)
            send_src(starts, 0)
            sq_buf[src] = placed(knot_squares())
            send_src(sq_buf, 1)
            wait_bytes(att_first, n_att - 1, att_recv.at[0])
            total = att_first[0]
            for j in range(1, n_att):
                total = total + att_first[j]
            source_inv = 1.0 / (total[count:] + damping)
            total = total[:count]
        else:
            pad = jnp.zeros((att_later.shape[2] - count, LANES), F32)
            att_later[turn - 1, att] = jnp.concatenate(terms + [pad], axis=0)
            send_att(att_later.at[turn - 1], turn)
            wait_bytes(att_later.at[turn - 1], n_att - 1, att_recv.at[turn])
            total = att_later[turn - 1, 0]
            for j in range(1, n_att):
                total = total + att_later[turn - 1, j]
            total = total[:count]
        x = x + total * source_inv
        grad_buf[turn, src] = placed(knot_terms(residual(x, predicted)))
        send_src(grad_buf.at[turn], 2 + turn)
        if turn == 0:
            wait_bytes(starts, n_src - 1, src_recv.at[0])
            if n_groups <= 2:
                for chunk in range(n_groups):
                    prepare(chunk, 0)
            else:
                lax.fori_loop(0, n_groups, prepare, 0)
            wait_bytes(sq_buf, n_src - 1, src_recv.at[1])
            inv[...] = 1.0 / (over_groups(lambda d: sq_buf[d]) + damping)
        if turn == PASSES - 1:
            for p in range(params):
                for b in range(blocks):
                    n = p * blocks + b
                    x_out[p : p + 1, b * LANES : (b + 1) * LANES] = x[n : n + 1, :]
        wait_bytes(grad_buf.at[turn], n_src - 1, src_recv.at[2 + turn])
        attitude = attitude + over_groups(lambda d: grad_buf[turn, d]) * inv[...]
    a_out[...] = attitude

    wait_bytes(att_first, n_att - 1, att_send.at[0])
    wait_bytes(starts, n_src - 1, src_send.at[0])
    wait_bytes(sq_buf, n_src - 1, src_send.at[1])
    for turn in range(PASSES):
        wait_bytes(grad_buf.at[turn], n_src - 1, src_send.at[2 + turn])
        if turn:
            wait_bytes(att_later.at[turn - 1], n_att - 1, att_send.at[turn])


def local(n_src, n_att, astro, attitude, spline_weights, source_coeffs, observations, knot_start, block_count):
    blocks = block_count.shape[1]
    params = astro.shape[0]
    tiles, knots, block_rows = spline_weights.shape
    slots = tiles // blocks
    knot_att = attitude.shape[0]
    rows = knot_att // LANES
    count = params * blocks
    vmem = pl.BlockSpec(memory_space=pltpu.VMEM)
    smem = pl.BlockSpec(memory_space=pltpu.SMEM)
    x, a = pl.pallas_call(
        functools.partial(kernel, n_src, n_att, blocks, slots, knots, params, rows),
        out_shape=(
            jax.ShapeDtypeStruct(astro.shape, F32),
            jax.ShapeDtypeStruct((rows, LANES), F32),
        ),
        in_specs=[vmem] * 6 + [smem],
        out_specs=(vmem, vmem),
        scratch_shapes=[
            pltpu.VMEM((params, tiles, LANES), F32),
            pltpu.VMEM((tiles, 8, LANES), F32),
            pltpu.VMEM((n_src // GROUP, rows, GROUP * tiles), BF16),
            pltpu.VMEM((2 * tiles, rows), BF16),
            pltpu.VMEM((n_src, tiles, LANES), jnp.int32),
            pltpu.VMEM((n_src, 8, LANES), jnp.int32),
            pltpu.VMEM((rows, 2 * LANES), F32),
            pltpu.VMEM((rows, LANES), F32),
            pltpu.VMEM((n_att, 2 * count, LANES), F32),
            pltpu.VMEM((PASSES - 1, n_att, (count + 7) // 8 * 8, LANES), F32),
            pltpu.VMEM((n_src, tiles // 2, LANES), F32),
            pltpu.VMEM((PASSES, n_src, tiles // 2, LANES), F32),
            pltpu.SemaphoreType.DMA((PASSES,)),
            pltpu.SemaphoreType.DMA((PASSES,)),
            pltpu.SemaphoreType.DMA((PASSES + 2,)),
            pltpu.SemaphoreType.DMA((PASSES + 2,)),
        ],
        compiler_params=pltpu.CompilerParams(
            collective_id=0, has_side_effects=True, vmem_limit_bytes=40 * 1024 * 1024
        ),
    )(
        astro,
        attitude.reshape(rows, LANES),
        spline_weights.reshape(tiles * knots, block_rows),
        source_coeffs,
        observations,
        knot_start.reshape(1, tiles),
        block_count,
    )
    return (x, a.reshape(knot_att))


def solution(mesh):
    placed_as = (
        P(None, "src"),
        P("att"),
        P(("src", "att"), None, None),
        P(("src", "att"), None, None),
        P(("src", "att"), None),
        P(("src", "att")),
        P("att", "src"),
    )
    return jax.shard_map(
        functools.partial(local, mesh.shape["src"], mesh.shape["att"]),
        mesh=mesh, in_specs=placed_as, out_specs=(P(None, "src"), P("att")), check_vma=False,
    )
```

```python
import functools

import jax
import jax.numpy as jnp
from jax import lax
from jax.experimental import pallas as pl
from jax.experimental.pallas import tpu as pltpu
from jax.sharding import PartitionSpec as P

PASSES = 2
LANES = 128
GROUP = 4

damping = 1.0

F32 = jnp.float32
BF16 = jnp.bfloat16
MESH = pl.DeviceIdType.MESH


def split(value):
    high = value.astype(BF16)
    low = (value - high.astype(F32)).astype(BF16)
    return high, low


def dot(a, b):
    return jnp.dot(a, b, preferred_element_type=F32)


def dot_rows(a, b):
    return lax.dot_general(a, b, (((1,), (1,)), ((), ())), preferred_element_type=F32)


def kernel(
    n_src, n_att, blocks, slots, knots, params, rows,
    astro_hbm, attitude_hbm, w_hbm, c_hbm, y_hbm, start_hbm, count_hbm,
    x_hbm, a_hbm,
    astro_ref, attitude_ref, w_ref, c_ref, y_ref, start_ref, count_ref, x_out, a_out, load_sem, store_sem,
    planes, hot, pick, offs, starts, acc, inv, att_buf, sq_buf, grad_buf,
    att_send, att_recv, src_send, src_recv,
):
    tiles = blocks * slots
    wide = slots * knots
    src = lax.axis_index("src")
    att = lax.axis_index("att")

    barrier = pltpu.get_barrier_semaphore()

    def each(n, step_fn):
        if n <= 8:
            for step in sorted(range(1, n), key=lambda step: min(step, n - step)):
                step_fn(step, 0)
        else:
            lax.fori_loop(1, n, step_fn, 0)

    def greet_src(step, carry):
        pl.semaphore_signal(barrier, inc=1, device_id=(lax.rem(src + step, n_src), att), device_id_type=MESH)
        return carry

    def greet_att(step, carry):
        pl.semaphore_signal(barrier, inc=1, device_id=(src, lax.rem(att + step, n_att)), device_id_type=MESH)
        return carry

    each(n_src, greet_src)
    each(n_att, greet_att)

    loads = [
        pltpu.make_async_copy(there, here, load_sem.at[n])
        for n, (there, here) in enumerate(
            [
                (start_hbm, start_ref), (attitude_hbm, attitude_ref), (w_hbm, w_ref), (c_hbm, c_ref),
                (count_hbm, count_ref), (y_hbm, y_ref), (astro_hbm, astro_ref),
            ]
        )
    ]
    for load in loads:
        load.start()

    def send_src(buf, which):
        def step_fn(step, carry):
            pltpu.make_async_remote_copy(
                src_ref=buf.at[src], dst_ref=buf.at[src],
                send_sem=src_send.at[which], recv_sem=src_recv.at[which],
                device_id=(lax.rem(src + step, n_src), att), device_id_type=MESH,
            ).start()
            return carry

        each(n_src, step_fn)

    def send_att(buf, which):
        def step_fn(step, carry):
            pltpu.make_async_remote_copy(
                src_ref=buf.at[att], dst_ref=buf.at[att],
                send_sem=att_send.at[which], recv_sem=att_recv.at[which],
                device_id=(src, lax.rem(att + step, n_att)), device_id_type=MESH,
            ).start()
            return carry

        each(n_att, step_fn)

    def wait_bytes(buf, count, sem):
        part = buf.at[pl.ds(0, count)]
        pltpu.make_async_copy(part, part, sem).wait()

    loads[0].wait()
    row_starts = start_ref[...]
    twice = jnp.broadcast_to(jnp.concatenate([row_starts, row_starts], axis=1), (8, LANES))
    starts[src] = twice
    column = jnp.transpose(twice)[0:tiles, 0:1]
    start = jnp.broadcast_to(column, (tiles, LANES))
    off = jnp.bitwise_and(start, LANES - 1)
    lane = lax.broadcasted_iota(jnp.int32, (tiles, LANES), 1)
    start_row = jnp.broadcast_to(jnp.right_shift(column, 7), (tiles, rows))
    row_id = lax.broadcasted_iota(jnp.int32, (tiles, rows), 1)
    pick[0:tiles, :] = jnp.where(row_id == start_row, 1.0, 0.0).astype(BF16)
    pick[tiles:, :] = jnp.where(row_id == start_row + 1, 1.0, 0.0).astype(BF16)

    loads[4].wait()
    slot_id = lax.broadcasted_iota(jnp.int32, (slots, LANES), 0)
    live = [slot_id < count_ref[0, b] for b in range(blocks)]
    own = jnp.right_shift(lax.broadcasted_iota(jnp.int32, (slots, wide), 1), 6) == lax.broadcasted_iota(
        jnp.int32, (slots, wide), 0
    )

    def windows(attitude):
        high, low = split(attitude)
        found = dot(pick[...], jnp.concatenate([high, low], axis=1))
        found = found[:, :LANES] + found[:, LANES:]
        window = jnp.where(lane >= off, found[:tiles], found[tiles:])
        covered = jnp.bitwise_and(lane - off, LANES - 1) < knots
        window = jnp.where(covered, window, pltpu.roll(window, knots, 1))
        for bit in range(6):
            moved = pltpu.roll(window, LANES - (1 << bit), 1)
            window = jnp.where(jnp.bitwise_and(off, 1 << bit) != 0, moved, window)
        return window

    def predict(window):
        found = []
        for b in range(blocks):
            part = window[b * slots : (b + 1) * slots]
            part = jnp.where(own, jnp.concatenate([part] * (wide // LANES), axis=1), 0.0)
            both = dot(jnp.concatenate(split(part), axis=0), w_ref[b * wide : (b + 1) * wide, :])
            found.append(both[:slots] + both[slots:])
        return found

    def residual(x, predicted):
        found = []
        for b in range(blocks):
            total = predicted[b]
            for p in range(params):
                total = total + planes[p, b * slots : (b + 1) * slots, :] * x[p * blocks + b : p * blocks + b + 1, :]
            found.append(jnp.where(live[b], y_ref[b * slots : (b + 1) * slots, :] - total, 0.0))
        return found

    def source_terms(resid):
        return [
            jnp.sum(planes[p, b * slots : (b + 1) * slots, :] * resid[b], axis=0, keepdims=True)
            for p in range(params)
            for b in range(blocks)
        ]

    def source_squares():
        return [
            jnp.sum(jnp.where(live[b], jnp.square(planes[p, b * slots : (b + 1) * slots, :]), 0.0), axis=0, keepdims=True)
            for p in range(params)
            for b in range(blocks)
        ]

    def own_columns(both):
        both = jnp.where(own, both[:slots] + both[slots:], 0.0)
        total = both[:, :LANES]
        for part in range(1, wide // LANES):
            total = total + both[:, part * LANES : (part + 1) * LANES]
        return total + pltpu.roll(total, knots, 1)

    def placed(values):
        values = jnp.concatenate(values, axis=0)
        for bit in range(6):
            moved = pltpu.roll(values, 1 << bit, 1)
            values = jnp.where(jnp.bitwise_and(off, 1 << bit) != 0, moved, values)
        half = tiles // 2
        return jnp.where(lane[:half] < knots, values[:half], values[half:])

    def knot_terms(resid):
        return [
            own_columns(dot_rows(jnp.concatenate(split(resid[b]), axis=0), w_ref[b * wide : (b + 1) * wide, :]))
            for b in range(blocks)
        ]

    def knot_squares():
        ones = jnp.ones((slots, LANES), BF16)
        found = []
        for b in range(blocks):
            high, low = split(jnp.square(w_ref[b * wide : (b + 1) * wide, :].astype(F32)))
            both = jnp.concatenate([dot_rows(ones, high), dot_rows(ones, low)], axis=0)
            found.append(jnp.where(live[b], own_columns(both), 0.0))
        return found

    def prepare(chunk, carry):
        first = chunk * GROUP
        low_half = lax.broadcasted_iota(jnp.int32, (8, LANES), 1) < tiles
        ids = lax.broadcasted_iota(jnp.int32, (rows, LANES), 0)
        for pair in range(GROUP // 2):
            both = jnp.where(low_half, starts[first + 2 * pair], starts[first + 2 * pair + 1])
            both = jnp.broadcast_to(jnp.right_shift(both, 7)[0:1], (rows, LANES))
            hot[chunk, :, pair * LANES : (pair + 1) * LANES] = jnp.where(ids == both, 1.0, 0.0).astype(BF16)
        for d in range(GROUP):
            lanes_of = jnp.transpose(jnp.bitwise_and(starts[first + d], LANES - 1))
            offs[first + d] = jnp.broadcast_to(lanes_of[0:tiles, 0:1], (tiles, LANES))
        return carry

    def group_sum(chunk, buf_of):
        first = chunk * GROUP
        half = tiles // 2
        parts = []
        for d in range(GROUP):
            packed = buf_of(first + d)
            other = pltpu.roll(packed, knots, 1)
            low_half = lane[:half] < knots
            values = jnp.concatenate([jnp.where(low_half, packed, other), jnp.where(low_half, other, packed)], axis=0)
            at = offs[first + d]
            here = jnp.where(jnp.logical_and(lane >= at, lane < at + knots), values, 0.0)
            later = jnp.where(lane < at - knots, values, 0.0)
            parts.append(jnp.concatenate([here, later], axis=1))
        high, low = split(jnp.concatenate(parts, axis=0))
        return dot(hot[chunk], high) + dot(hot[chunk], low)

    n_groups = n_src // GROUP

    def over_groups(buf_of):
        if n_groups <= 2:
            total = group_sum(0, buf_of)
            for chunk in range(1, n_groups):
                total = total + group_sum(chunk, buf_of)
        else:
            acc[...] = jnp.zeros_like(acc)

            def step_fn(chunk, carry):
                acc[...] += group_sum(chunk, buf_of)
                return carry

            lax.fori_loop(0, n_groups, step_fn, 0)
            total = acc[...]
        return total[:, :LANES] + pltpu.roll(total[:, LANES:], 1, 0)

    stores = [
        pltpu.make_async_copy(x_out, x_hbm, store_sem.at[0]),
        pltpu.make_async_copy(a_out, a_hbm, store_sem.at[1]),
    ]
    count = params * blocks
    pad = jnp.zeros((att_buf.shape[2] - count, LANES), F32)

    def att_total(which):
        wait_bytes(att_buf.at[which], n_att - 1, att_recv.at[which])
        total = att_buf[which, 0]
        for j in range(1, n_att):
            total = total + att_buf[which, j]
        return total[:count]

    loads[1].wait()
    window = windows(attitude_ref[...])
    for n in (2, 3, 5, 6):
        loads[n].wait()
    for p in range(params):
        planes[p] = c_ref[p].astype(F32)
    x = jnp.concatenate(
        [astro_ref[p : p + 1, b * LANES : (b + 1) * LANES] for p in range(params) for b in range(blocks)], axis=0
    )
    attitude = attitude_ref[...]
    for turn in range(PASSES):
        predicted = predict(window)
        terms = source_terms(residual(x, predicted))
        att_buf[turn, att] = jnp.concatenate(terms + [pad], axis=0)
        if turn == 0:
            pl.semaphore_wait(barrier, n_src + n_att - 2)
        send_att(att_buf.at[turn], turn)
        if turn == 0:
            att_buf[PASSES, att] = jnp.concatenate(source_squares() + [pad], axis=0)
            send_att(att_buf.at[PASSES], PASSES)
            send_src(starts, 0)
            sq_buf[src] = placed(knot_squares())
            send_src(sq_buf, 1)
            source_inv = 1.0 / (att_total(PASSES) + damping)
        total = att_total(turn)
        x = x + total * source_inv
        grad_buf[turn, src] = placed(knot_terms(residual(x, predicted)))
        send_src(grad_buf.at[turn], 2 + turn)
        if turn == 0:
            wait_bytes(starts, n_src - 1, src_recv.at[0])
            if n_groups <= 2:
                for chunk in range(n_groups):
                    prepare(chunk, 0)
            else:
                lax.fori_loop(0, n_groups, prepare, 0)
            wait_bytes(sq_buf, n_src - 1, src_recv.at[1])
            inv[...] = 1.0 / (over_groups(lambda d: sq_buf[d]) + damping)
        if turn == PASSES - 1:
            for p in range(params):
                for b in range(blocks):
                    n = p * blocks + b
                    x_out[p : p + 1, b * LANES : (b + 1) * LANES] = x[n : n + 1, :]
            stores[0].start()
        wait_bytes(grad_buf.at[turn], n_src - 1, src_recv.at[2 + turn])
        attitude = attitude + over_groups(lambda d: grad_buf[turn, d]) * inv[...]
        if turn < PASSES - 1:
            window = windows(attitude)
    a_out[...] = attitude
    stores[1].start()

    wait_bytes(starts, n_src - 1, src_send.at[0])
    wait_bytes(sq_buf, n_src - 1, src_send.at[1])
    wait_bytes(att_buf.at[PASSES], n_att - 1, att_send.at[PASSES])
    for turn in range(PASSES):
        wait_bytes(att_buf.at[turn], n_att - 1, att_send.at[turn])
        wait_bytes(grad_buf.at[turn], n_src - 1, src_send.at[2 + turn])
    for store in stores:
        store.wait()


def local(n_src, n_att, astro, attitude, spline_weights, source_coeffs, observations, knot_start, block_count):
    blocks = block_count.shape[1]
    params = astro.shape[0]
    tiles, knots, block_rows = spline_weights.shape
    slots = tiles // blocks
    knot_att = attitude.shape[0]
    rows = knot_att // LANES
    count = params * blocks
    hbm = pl.BlockSpec(memory_space=pltpu.HBM)
    x, a = pl.pallas_call(
        functools.partial(kernel, n_src, n_att, blocks, slots, knots, params, rows),
        out_shape=(
            jax.ShapeDtypeStruct(astro.shape, F32),
            jax.ShapeDtypeStruct((rows, LANES), F32),
        ),
        in_specs=[hbm] * 7,
        out_specs=(hbm, hbm),
        scratch_shapes=[
            pltpu.VMEM(astro.shape, F32),
            pltpu.VMEM((rows, LANES), F32),
            pltpu.VMEM((tiles * knots, block_rows), BF16),
            pltpu.VMEM((params, tiles, block_rows), BF16),
            pltpu.VMEM((tiles, block_rows), F32),
            pltpu.VMEM((1, tiles), jnp.int32),
            pltpu.SMEM((1, blocks), jnp.int32),
            pltpu.VMEM(astro.shape, F32),
            pltpu.VMEM((rows, LANES), F32),
            pltpu.SemaphoreType.DMA((7,)),
            pltpu.SemaphoreType.DMA((2,)),
            pltpu.VMEM((params, tiles, LANES), F32),
            pltpu.VMEM((n_src // GROUP, rows, GROUP * tiles), BF16),
            pltpu.VMEM((2 * tiles, rows), BF16),
            pltpu.VMEM((n_src, tiles, LANES), jnp.int32),
            pltpu.VMEM((n_src, 8, LANES), jnp.int32),
            pltpu.VMEM((rows, 2 * LANES), F32),
            pltpu.VMEM((rows, LANES), F32),
            pltpu.VMEM((PASSES + 1, n_att, (count + 7) // 8 * 8, LANES), F32),
            pltpu.VMEM((n_src, tiles // 2, LANES), F32),
            pltpu.VMEM((PASSES, n_src, tiles // 2, LANES), F32),
            pltpu.SemaphoreType.DMA((PASSES + 1,)),
            pltpu.SemaphoreType.DMA((PASSES + 1,)),
            pltpu.SemaphoreType.DMA((PASSES + 2,)),
            pltpu.SemaphoreType.DMA((PASSES + 2,)),
        ],
        compiler_params=pltpu.CompilerParams(
            collective_id=0, has_side_effects=True, vmem_limit_bytes=60 * 1024 * 1024
        ),
    )(
        astro,
        attitude.reshape(rows, LANES),
        spline_weights.reshape(tiles * knots, block_rows),
        jnp.transpose(source_coeffs, (1, 0, 2)),
        observations,
        knot_start.reshape(1, tiles),
        block_count,
    )
    return (x, a.reshape(knot_att))


def solution(mesh):
    placed_as = (
        P(None, "src"),
        P("att"),
        P(("src", "att"), None, None),
        P(("src", "att"), None, None),
        P(("src", "att"), None),
        P(("src", "att")),
        P("att", "src"),
    )
    return jax.shard_map(
        functools.partial(local, mesh.shape["src"], mesh.shape["att"]),
        mesh=mesh, in_specs=placed_as, out_specs=(P(None, "src"), P("att")), check_vma=False,
    )
```
